32 devices in a mesh: grp: 2 (over x), row: 16 (over z, y, core).
Axes of the slice: x: 2, y: 2, z: 4, core: 2. Of those that a mesh axis runs over, the one named last changes fastest.
Arguments:
- sources: bfloat16 [32, 8, 8, 1024], P(('grp', 'row')), parts along dimension 0, may hold values from -6 to 6
- far_left: bfloat16 [64, 15, 48, 1024], P(('grp', 'row')), parts along dimension 0, may hold values from -0.1875 to 0.1875
- far_right: bfloat16 [64, 15, 48, 1024], P(('grp', 'row')), parts along dimension 0, may hold values from -0.078125 to 0.078125
- ranks: int32 [64, 15], P(('grp', 'row')), parts along dimension 0, may hold values from 16 to 48
- near_blocks: bfloat16 [6, 1024, 1024], P('grp'), parts along dimension 0, may hold values from -0.1875 to 0.1875
- near_offsets: int32 [6, 2], P('grp'), parts along dimension 0, may hold values from -1 to 1, as said below
Outputs:
- fields: float32 [32, 8, 8, 1024], P(('grp', 'row')), parts along dimension 0
The draws below stay inside these ranges and needn't reach their ends.
There are 2 independent parts, one for each index of `grp`. The reference program is written for one: setup_inputs(seed, part) draws one part's arguments, and reference() takes and returns one part's arrays. A program takes and returns all parts, laid end to end along the dimension named above; each array names one. Nothing has to cross between parts.
Inputs may be any that keep to these rules, and one draw needn't show every extreme that they name: `near_offsets`: the rows are 3 distinct offsets (a, b); row 0 is the self offset (0, 0).
All inputs are finite; a program needn't handle non-finite values.
Results may differ from the reference program's by a relative error of at most 0.0014.
Values may be sent and summed in bfloat16 or wider, within the bound.
A program may use at most 64 MiB of HBM per device.

```python
import jax
import jax.numpy as jnp
from jax import lax

NB = 1024
RANK = 48
ECOL = 8
BEAMS = 8
NNEAR = 3
ROWS = 16
SLOTS = 15


def draw_ranks(key, part):
    values = jax.random.randint(key, (2 * ROWS * SLOTS,), RANK // 3, RANK + 1)
    chosen = jax.random.randint(jax.random.fold_in(key, 7), (), 0, 2 * ROWS * SLOTS)
    values = jnp.where(jnp.arange(2 * ROWS * SLOTS) == chosen, RANK, values)
    return values.reshape(2 * ROWS, SLOTS).astype(jnp.int32)


def draw_near_offsets(key, part):
    others = jax.random.permutation(jax.random.fold_in(key, 11), 8)[:NNEAR - 1]
    others = others + (others >= 4).astype(others.dtype)
    picks = jnp.concatenate([jnp.array([4], dtype=others.dtype), others])
    return jnp.stack([picks // 3 - 1, picks % 3 - 1], axis=1).astype(jnp.int32)


def block_scale(rng, extent, shards, least, top_value):
    def one(axis_at, parts):
        steps = jax.random.uniform(jax.random.fold_in(jax.random.fold_in(rng, 6), axis_at), (parts,), jnp.float32, least / len(shards), top_value / len(shards))
        return jnp.repeat(jnp.exp(steps), extent[axis_at] // parts).reshape((-1,) + (1,) * (len(extent) - axis_at - 1))

    factor_of = one(*shards[0])
    for cut in shards[1:]:
        factor_of = factor_of * one(*cut)
    return factor_of


def scatter_about(key, dims, scale, limit, shards=(), held_as=jnp.bfloat16):
    factor_of = block_scale(key, dims, shards, -0.22, 0.18) if shards else 1.0
    values = jax.random.normal(key, dims, jnp.float32) * scale * factor_of
    return jnp.minimum(jnp.maximum(values, -limit), limit).astype(held_as)


def setup_inputs(seed: int = 0, part: int = 0) -> dict:
    seeds = jax.random.split(jax.random.key(seed), 7)
    part_keys = jax.random.split(jax.random.fold_in(seeds[6], part), 7)
    return {
        "sources": scatter_about(part_keys[0], (ROWS, ECOL, BEAMS, NB), 1.0, 6.0, ((0, 16),)),
        "far_left": scatter_about(part_keys[1], (2 * ROWS, SLOTS, RANK, NB), NB ** -0.5, 0.1875, ((0, 16),)),
        "far_right": scatter_about(part_keys[2], (2 * ROWS, SLOTS, RANK, NB), (ROWS * ECOL * RANK) ** -0.5, 0.078125, ((0, 16),)),
        "ranks": draw_ranks(jax.random.fold_in(jax.random.fold_in(seeds[6], part), 71), part),
        "near_blocks": scatter_about(part_keys[4], (NNEAR, NB, NB), NB ** -0.5, 0.1875),
        "near_offsets": draw_near_offsets(jax.random.fold_in(jax.random.fold_in(seeds[6], part), 71), part),
    }


def slot_mask(rank_row, row_offset, near_offsets):
    col_offset = jnp.arange(SLOTS, dtype=jnp.int32) - (ECOL - 1)
    hit = jnp.any((near_offsets[:, 0][:, None] == row_offset) & (near_offsets[:, 1][:, None] == col_offset[None, :]), axis=0)
    live = jnp.arange(RANK, dtype=jnp.int32)[None, :] < rank_row[:, None]
    return (live & jnp.logical_not(hit)[:, None]).astype(jnp.float32)


def spread(coeffs):
    rank_dims = coeffs.ndim
    pads = [(0, 0)] * rank_dims
    pads[rank_dims - 4] = (ECOL, ECOL)
    padded = jnp.pad(coeffs, pads)
    columns = [padded[..., 2 * ECOL - 1 - k:3 * ECOL - 1 - k, k, :, :] for k in range(SLOTS)]
    return jnp.stack(columns, axis=-3)


def reference(sources, far_left, far_right, ranks, near_blocks, near_offsets):
    zero_rows = jnp.zeros((ROWS, ECOL, BEAMS, NB), jnp.bfloat16)
    padded = jnp.concatenate([zero_rows, sources, zero_rows], axis=0)

    def add_slot(slot, total):
        dist = slot // 2
        wrap_bit = slot % 2
        row_offset = (dist - ROWS * wrap_bit).astype(jnp.int32)
        shifted = lax.dynamic_slice_in_dim(padded, (ROWS - row_offset).astype(jnp.int32), ROWS, 0)
        keep = slot_mask(ranks[slot], row_offset, near_offsets)
        coeffs = jnp.einsum('tsbn,krn->tskbr', shifted.astype(jnp.float32), far_left[slot].astype(jnp.float32))
        coeffs = coeffs * keep[None, None, :, None, :]
        coeffs = lax.optimization_barrier(coeffs.astype(jnp.bfloat16)).astype(jnp.float32)
        return total + jnp.einsum('tjkbr,krn->tjbn', spread(coeffs), far_right[slot].astype(jnp.float32))

    far = lax.fori_loop(0, 2 * ROWS, add_slot, jnp.zeros((ROWS, ECOL, BEAMS, NB), jnp.float32))
    both_pad = jnp.pad(sources, ((1, 1), (1, 1), (0, 0), (0, 0)))
    near = jnp.zeros((ROWS, ECOL, BEAMS, NB), jnp.float32)
    for index in range(NNEAR):
        row_offset = near_offsets[index, 0]
        col_offset = near_offsets[index, 1]
        start = ((1 - row_offset).astype(jnp.int32), (1 - col_offset).astype(jnp.int32), jnp.int32(0), jnp.int32(0))
        shifted = lax.dynamic_slice(both_pad, start, (ROWS, ECOL, BEAMS, NB))
        term = jnp.dot(shifted.reshape(-1, NB), near_blocks[index], preferred_element_type=jnp.float32)
        near = near + term.reshape(ROWS, ECOL, BEAMS, NB)
    return near + far
```

```python
import functools

import jax
import jax.numpy as jnp
from jax import lax
from jax.experimental import pallas as pl
from jax.experimental.pallas import tpu as pltpu
from jax.sharding import PartitionSpec as P

MESH = pl.DeviceIdType.MESH
F32 = jnp.float32
BF16 = jnp.bfloat16
LANES = 128


def kernel(
    dims,
    src, left_hbm, right_hbm, near_hbm, ranks, offsets,
    out,
    rows_all, left, right, near_w, coeff_pad, spread_all, partial, sib_in,
    ring_out, ring_in, beside, keep, near_acc,
    load_sem, g_send, g_recv, gs_send, gs_recv, r_send, r_recv, rs_send, rs_recv,
):
    count, ecol, beams, width, slots, rank, depth, nnear = dims
    chips = count // 2
    half_ring = chips // 2
    rows = ecol * beams
    half = rows // 2
    used = slots * rank

    me = lax.axis_index("row")
    core = me % 2
    chip = me // 2
    pos = (1 - chip % 2) * (chip // 2) + (chip % 2) * (chips - 1 - chip // 2)

    def chip_at(place):
        place = (place + 2 * chips) % chips
        upper = place // half_ring
        return (1 - upper) * 2 * place + upper * (2 * (chips - 1 - place) + 1)

    def row_at(place):
        return 2 * chip_at(place) + core

    ahead = row_at(pos + 1)
    behind = row_at(pos - 1)
    sibling = me + 1 - 2 * core

    def send(source, target, send_sem, recv_sem, device):
        return pltpu.make_async_remote_copy(
            src_ref=source, dst_ref=target, send_sem=send_sem, recv_sem=recv_sem,
            device_id={"row": device}, device_id_type=MESH,
        )

    loads = [pltpu.make_async_copy(src, rows_all.at[me], load_sem.at[0])]
    for w in range(2):
        loads.append(pltpu.make_async_copy(
            left_hbm.at[w], left.at[w, pl.ds(0, used)], load_sem.at[1 + w]))
        loads.append(pltpu.make_async_copy(
            right_hbm.at[w], right.at[w, pl.ds(0, used)], load_sem.at[3 + w]))
    loads.append(pltpu.make_async_copy(near_hbm, near_w, load_sem.at[5]))

    barrier = pltpu.get_barrier_semaphore()
    for device in (ahead, behind, sibling):
        pl.semaphore_signal(barrier, inc=1, device_id={"row": device}, device_id_type=MESH)
    loads[0].start()
    loads[1].start()
    loads[3].start()
    pl.semaphore_wait(barrier, 3)

    def part(ref, lead, h):
        return ref.at[lead, pl.ds(h * half, half)]

    def hop(way, step, h, row, source=None):
        block = part(rows_all, row, h)
        return send(
            block if source is None else source, block,
            g_send.at[way, step - 1, h], g_recv.at[way, step - 1, h],
            ahead if way == 0 else behind,
        )

    def cross(index, h, row, source=None):
        block = part(rows_all, row, h)
        return send(
            block if source is None else source, block,
            gs_send.at[index, h], gs_recv.at[index, h], sibling,
        )

    for h in range(2):
        mine = src.at[pl.ds(h * half, half)]
        hop(0, 1, h, me, mine).start()
        hop(1, 1, h, me, mine).start()
        cross(0, h, me, mine).start()
    loads[2].start()
    loads[4].start()
    loads[5].start()

    for w in range(2):
        left[w, pl.ds(used, depth - used), :] = jnp.zeros((depth - used, width), BF16)
        right[w, pl.ds(used, depth - used), :] = jnp.zeros((depth - used, width), BF16)
    for i in range(2):
        coeff_pad[i, pl.ds(0, rows), :] = jnp.zeros((rows, depth), F32)
        coeff_pad[i, pl.ds(2 * rows, rows), :] = jnp.zeros((rows, depth), F32)
    lane = lax.broadcasted_iota(jnp.int32, (8, depth), 1)
    for w in range(2):
        top = jnp.zeros((8, depth), jnp.int32)
        for k in range(slots):
            free = jnp.int32(1)
            for n in range(nnear):
                rows_off = offsets[n, 0] - (me - count * w)
                cols_off = offsets[n, 1] - (k - (ecol - 1))
                free = free * jnp.minimum(rows_off * rows_off + cols_off * cols_off, 1)
            level = rank * k + ranks[w, k] * free
            top = jnp.where(lane >= rank * k, level, top)
        top = jnp.where(lane < used, top, 0)
        keep[w] = jnp.clip(top - lane, 0, 1).astype(F32)

    tile_lane = lax.broadcasted_iota(jnp.int32, (rows, LANES), 1)

    def wrap(source):
        return (source + me) // count

    def coeffs_of(place):
        first = 2 * chip_at(place)
        block = rows_all[pl.ds(first, 2)].reshape(2 * rows, width)

        def one(w, carry):
            product = lax.dot_general(
                block, left[w], (((1,), (1,)), ((), ())), preferred_element_type=F32)
            mask = keep[w][0:1, :]
            for i in range(2):
                @pl.when(wrap(first + i) == w)
                def _():
                    coeff_pad[i, pl.ds(rows, rows), :] = (
                        product[i * rows:(i + 1) * rows, :] * mask)
            return carry

        lax.fori_loop(wrap(first), wrap(first + 1) + 1, one, 0)
        for i in range(2):
            target = (first + i + me) % count
            for tile in range(depth // LANES):
                low = tile * LANES
                first_k = min(low // rank, slots - 1)
                last_k = min((low + LANES - 1) // rank, slots - 1)
                value = None
                for k in range(first_k, last_k + 1):
                    start = rows + (ecol - 1 - k) * beams
                    piece = coeff_pad[i, pl.ds(start, rows), pl.ds(low, LANES)]
                    if value is None:
                        value = piece
                    else:
                        value = jnp.where(tile_lane >= rank * k - low, piece, value)
                spread_all[target, :, pl.ds(low, LANES)] = value.astype(BF16)

    def take(step, all_on):
        for h in range(2):
            for way in range(2):
                row = row_at(pos - step if way == 0 else pos + step)
                index = chips - step if way == 0 else step
                hop(way, step, h, row).wait_recv()
                if all_on or h == way:
                    hop(way, step + 1, h, row).start()
                cross(index, h, row).start()

    def cross_arrived(index, place):
        other = 2 * chip_at(place) + 1 - core
        for h in range(2):
            cross(index, h, other).wait_recv()

    def both_coeffs(step):
        def one(way, carry):
            index = (1 - way) * (chips - step) + way * step
            cross_arrived(index, pos + index)
            coeffs_of(pos + index)
            return carry
        lax.fori_loop(0, 2, one, 0)

    def gather_step(step, carry):
        take(step, True)

        @pl.when(step == 1)
        def _():
            loads[0].wait()
            loads[1].wait()
            loads[3].wait()
            cross_arrived(0, pos)
            coeffs_of(pos)

        @pl.when(step > 1)
        def _():
            both_coeffs(step - 1)
        return carry

    lax.fori_loop(1, half_ring - 1, gather_step, 0)
    take(half_ring - 1, False)
    both_coeffs(half_ring - 2)
    for way in range(2):
        hop(way, half_ring, way, row_at(pos + half_ring)).wait_recv()
        cross(half_ring, way, row_at(pos + half_ring)).start()
    both_coeffs(half_ring - 1)
    cross_arrived(half_ring, pos + half_ring)
    coeffs_of(pos + half_ring)

    def behind_me(target):
        return (target < me).astype(jnp.int32)

    def cross_sum(index):
        return send(
            partial.at[index, 1 - core], sib_in.at[index],
            rs_send.at[index], rs_recv.at[index], sibling)

    def fields_of(index):
        first = 2 * chip_at(pos + index)
        block = spread_all[pl.ds(first, 2)].reshape(2 * rows, depth)

        def one(w, carry):
            product = jnp.dot(block, right[w], preferred_element_type=F32)
            for i in range(2):
                @pl.when(behind_me(first + i) == w)
                def _():
                    partial[index, i] = product[i * rows:(i + 1) * rows, :]
            return carry

        lax.fori_loop(behind_me(first + 1), behind_me(first) + 1, one, 0)
        cross_sum(index).start()

    def both_fields(distance):
        def one(way, carry):
            fields_of((1 - way) * distance + way * (chips - distance))
            return carry
        lax.fori_loop(0, 2, one, 0)

    def ring(way, step, h):
        return send(
            ring_out.at[way, step - 1, pl.ds(h * half, half)],
            ring_in.at[way, step - 1, pl.ds(h * half, half)],
            r_send.at[way, step - 1, h], r_recv.at[way, step - 1, h],
            ahead if way == 0 else behind,
        )

    def own(index, h):
        at = pl.ds(h * half, half)
        return partial[index, core, at, :] + sib_in[index, at, :]

    def pass_on(step, way, h, fresh):
        distance = half_ring - (step - 1)
        index = distance if way == 0 else chips - distance
        at = pl.ds(h * half, half)
        total = own(index, h)
        if not fresh:
            ring(way, step - 1, h).wait_recv()
            total = total + ring_in[way, step - 2, at, :].astype(F32)
        ring_out[way, step - 1, at, :] = total.astype(ring_out.dtype)
        ring(way, step, h).start()

    loads[2].wait()
    loads[4].wait()
    fields_of(half_ring)
    both_fields(half_ring - 1)
    cross_sum(half_ring).wait_recv()
    pass_on(1, 0, 0, True)
    pass_on(1, 1, 1, True)
    cross_sum(half_ring - 1).wait_recv()
    cross_sum(chips - half_ring + 1).wait_recv()
    pass_on(2, 0, 1, True)
    pass_on(2, 1, 0, True)
    both_fields(half_ring - 2)
    pass_on(2, 0, 0, False)
    pass_on(2, 1, 1, False)

    def reduce_step(step, carry):
        distance = half_ring - step

        @pl.when(distance > 0)
        def _():
            both_fields(distance)
        cross_sum(distance + 1).wait_recv()
        cross_sum(chips - distance - 1).wait_recv()
        pass_on(step, 0, 1, False)
        pass_on(step, 1, 0, False)
        pass_on(step, 0, 0, False)
        pass_on(step, 1, 1, False)
        return carry

    lax.fori_loop(3, half_ring + 1, reduce_step, 0)
    fields_of(0)

    loads[5].wait()
    for i in range(3):
        row = me + i - 1
        inside = jnp.logical_and(row >= 0, row < count)
        block = rows_all[(row + count) % count].astype(F32)
        beside[i, pl.ds(0, beams), :] = jnp.zeros((beams, width), F32)
        beside[i, pl.ds(beams, rows), :] = jnp.where(inside, block, 0.0)
        beside[i, pl.ds(beams + rows, beams), :] = jnp.zeros((beams, width), F32)
    near_acc[...] = jnp.zeros((rows, width), F32)

    def weights(offset):
        square = offset * offset
        return [((square + offset) // 2).astype(F32), (1 - square).astype(F32),
                ((square - offset) // 2).astype(F32)]

    def near_step(n, carry):
        by_row = weights(offsets[n, 0])
        by_col = weights(offsets[n, 1])
        picked = sum(beside[i] * by_row[i] for i in range(3))
        shifted = sum(
            picked[i * beams:i * beams + rows, :] * by_col[i] for i in range(3)).astype(BF16)
        near_acc[...] += jnp.dot(shifted, near_w[n], preferred_element_type=F32)
        return carry

    lax.fori_loop(0, nnear, near_step, 0)

    cross_sum(0).wait_recv()
    for h in range(2):
        at = pl.ds(h * half, half)
        total = near_acc[at, :] + own(0, h)
        for way in range(2):
            ring(way, half_ring, h).wait_recv()
            total = total + ring_in[way, half_ring - 1, at, :].astype(F32)
        out[at, :] = total

    def sent(step, carry):
        for way in range(2):
            for h in range(2):
                hop(way, step, h, me).wait_send()
                ring(way, half_ring + 1 - step, h).wait_send()
        return carry

    lax.fori_loop(1, half_ring, sent, 0)
    for way in range(2):
        hop(way, half_ring, way, me).wait_send()
        ring(way, 1, way).wait_send()

    def crossed(index, carry):
        for h in range(2):
            cross(index, h, me).wait_send()
        cross_sum(index).wait_send()
        return carry

    lax.fori_loop(0, chips, crossed, 0)


def local(count, sources, far_left, far_right, ranks, near_blocks, near_offsets):
    _, ecol, beams, width = sources.shape
    slots, rank = far_left.shape[1], far_left.shape[2]
    nnear = near_blocks.shape[0]
    chips, rows = count // 2, ecol * beams
    half_ring = chips // 2
    depth = -(-slots * rank // 256) * 256
    dims = (count, ecol, beams, width, slots, rank, depth, nnear)
    flops = 2 * count * rows * depth * width * 2 + 2 * nnear * rows * width * width
    dma = pltpu.SemaphoreType.DMA
    anywhere = pl.BlockSpec(memory_space=pl.ANY)
    scalars = pl.BlockSpec(memory_space=pltpu.SMEM)
    fields = pl.pallas_call(
        functools.partial(kernel, dims),
        out_shape=jax.ShapeDtypeStruct((rows, width), F32),
        in_specs=[anywhere] * 4 + [scalars] * 2,
        out_specs=pl.BlockSpec(memory_space=pltpu.VMEM),
        scratch_shapes=[
            pltpu.VMEM((count, rows, width), BF16),
            pltpu.VMEM((2, depth, width), BF16),
            pltpu.VMEM((2, depth, width), BF16),
            pltpu.VMEM((nnear, width, width), BF16),
            pltpu.VMEM((2, 3 * rows, depth), F32),
            pltpu.VMEM((count, rows, depth), BF16),
            pltpu.VMEM((chips, 2, rows, width), F32),
            pltpu.VMEM((chips, rows, width), F32),
            pltpu.VMEM((2, half_ring, rows, width), BF16),
            pltpu.VMEM((2, half_ring, rows, width), BF16),
            pltpu.VMEM((3, rows + 2 * beams, width), F32),
            pltpu.VMEM((2, 8, depth), F32),
            pltpu.VMEM((rows, width), F32),
            dma((6,)),
            dma((2, half_ring, 2)),
            dma((2, half_ring, 2)),
            dma((chips, 2)),
            dma((chips, 2)),
            dma((2, half_ring, 2)),
            dma((2, half_ring, 2)),
            dma((chips,)),
            dma((chips,)),
        ],
        compiler_params=pltpu.CompilerParams(
            collective_id=0, has_side_effects=True, vmem_limit_bytes=62 * 2 ** 20),
        cost_estimate=pl.CostEstimate(
            flops=flops, bytes_accessed=13_000_000, transcendentals=0),
    )(
        sources.reshape(rows, width),
        far_left.reshape(2, slots * rank, width),
        far_right.reshape(2, slots * rank, width),
        near_blocks, ranks, near_offsets,
    )
    return fields.reshape(1, ecol, beams, width)


def solution(mesh):
    placed = (
        P(("grp", "row"), None, None, None),
        P(("grp", "row"), None, None, None),
        P(("grp", "row"), None, None, None),
        P(("grp", "row"), None),
        P("grp", None, None),
        P("grp", None),
    )
    return jax.shard_map(
        functools.partial(local, mesh.shape["row"]),
        mesh=mesh,
        in_specs=placed,
        out_specs=P(("grp", "row"), None, None, None),
        check_vma=False,
    )
```

```python
import functools

import jax
import jax.numpy as jnp
from jax import lax
from jax.experimental import pallas as pl
from jax.experimental.pallas import tpu as pltpu
from jax.sharding import PartitionSpec as P

MESH = pl.DeviceIdType.MESH
PARTS = 4
ORDER = ((0, 1, 2, 3), (2, 3, 0, 1))
F32 = jnp.float32
BF16 = jnp.bfloat16
LANES = 128


def kernel(
    dims,
    src, left_hbm, right_hbm, near_hbm, ranks, offsets,
    out,
    rows_all, left, right, near_w, coeff_pad, spread_all, partial, sib_in,
    ring_out, ring_in, beside, keep, near_acc,
    load_sem, g_send, g_recv, gs_send, gs_recv, r_send, r_recv, rs_send, rs_recv,
):
    count, ecol, beams, width, slots, rank, depth, nnear = dims
    chips = count // 2
    half_ring = chips // 2
    rows = ecol * beams
    half = rows // PARTS
    used = slots * rank

    me = lax.axis_index("row")
    core = me % 2
    chip = me // 2
    pos = (1 - chip % 2) * (chip // 2) + (chip % 2) * (chips - 1 - chip // 2)

    def chip_at(place):
        place = (place + 2 * chips) % chips
        upper = place // half_ring
        return (1 - upper) * 2 * place + upper * (2 * (chips - 1 - place) + 1)

    def row_at(place):
        return 2 * chip_at(place) + core

    ahead = row_at(pos + 1)
    behind = row_at(pos - 1)
    sibling = me + 1 - 2 * core

    def send(source, target, send_sem, recv_sem, device):
        return pltpu.make_async_remote_copy(
            src_ref=source, dst_ref=target, send_sem=send_sem, recv_sem=recv_sem,
            device_id={"row": device}, device_id_type=MESH,
        )

    loads = [pltpu.make_async_copy(src, rows_all.at[me], load_sem.at[0])]
    for w in range(2):
        loads.append(pltpu.make_async_copy(
            left_hbm.at[w], left.at[w, pl.ds(0, used)], load_sem.at[1 + w]))
        loads.append(pltpu.make_async_copy(
            right_hbm.at[w], right.at[w, pl.ds(0, used)], load_sem.at[3 + w]))
    loads.append(pltpu.make_async_copy(near_hbm, near_w, load_sem.at[5]))

    barrier = pltpu.get_barrier_semaphore()
    for device in (ahead, behind, sibling):
        pl.semaphore_signal(barrier, inc=1, device_id={"row": device}, device_id_type=MESH)
    loads[0].start()
    loads[1].start()
    loads[3].start()
    loads[2].start()
    loads[4].start()
    loads[5].start()
    pl.semaphore_wait(barrier, 3)

    def part(ref, lead, h):
        return ref.at[lead, pl.ds(h * half, half)]

    def hop(way, step, h, row):
        block = part(rows_all, row, h)
        return send(
            block, block,
            g_send.at[way, step - 1, h], g_recv.at[way, step - 1, h],
            ahead if way == 0 else behind,
        )

    def cross(index, h, row):
        block = part(rows_all, row, h)
        return send(
            block, block, gs_send.at[index, h], gs_recv.at[index, h], sibling,
        )

    loads[0].wait()
    for i in range(PARTS):
        for way in range(2):
            hop(way, 1, ORDER[way][i], me).start()
    for h in range(PARTS):
        cross(0, h, me).start()

    for w in range(2):
        left[w, pl.ds(used, depth - used), :] = jnp.zeros((depth - used, width), BF16)
        right[w, pl.ds(used, depth - used), :] = jnp.zeros((depth - used, width), BF16)
    for i in range(2):
        coeff_pad[i, pl.ds(0, rows), :] = jnp.zeros((rows, depth), F32)
        coeff_pad[i, pl.ds(2 * rows, rows), :] = jnp.zeros((rows, depth), F32)
    lane = lax.broadcasted_iota(jnp.int32, (8, depth), 1)
    for w in range(2):
        top = jnp.zeros((8, depth), jnp.int32)
        for k in range(slots):
            free = jnp.int32(1)
            for n in range(nnear):
                rows_off = offsets[0, n] - (me - count * w)
                cols_off = offsets[1, n] - (k - (ecol - 1))
                free = free * jnp.minimum(rows_off * rows_off + cols_off * cols_off, 1)
            level = rank * k + ranks[w, k] * free
            top = jnp.where(lane >= rank * k, level, top)
        top = jnp.where(lane < used, top, 0)
        keep[w] = jnp.clip(top - lane, 0, 1).astype(F32)

    tile_lane = lax.broadcasted_iota(jnp.int32, (rows, LANES), 1)

    def wrap(source):
        return (source + me) // count

    def coeffs_of(place):
        first = 2 * chip_at(place)
        block = rows_all[pl.ds(first, 2)].reshape(2 * rows, width)

        def one(w, carry):
            product = lax.dot_general(
                block, left[w], (((1,), (1,)), ((), ())), preferred_element_type=F32)
            mask = keep[w][0:1, :]
            for i in range(2):
                @pl.when(wrap(first + i) == w)
                def _():
                    coeff_pad[i, pl.ds(rows, rows), :] = (
                        product[i * rows:(i + 1) * rows, :] * mask)
            return carry

        lax.fori_loop(wrap(first), wrap(first + 1) + 1, one, 0)
        for i in range(2):
            target = (first + i + me) % count
            for tile in range(depth // LANES):
                low = tile * LANES
                first_k = min(low // rank, slots - 1)
                last_k = min((low + LANES - 1) // rank, slots - 1)
                value = None
                for k in range(first_k, last_k + 1):
                    start = rows + (ecol - 1 - k) * beams
                    piece = coeff_pad[i, pl.ds(start, rows), pl.ds(low, LANES)]
                    if value is None:
                        value = piece
                    else:
                        value = jnp.where(tile_lane >= rank * k - low, piece, value)
                spread_all[target, :, pl.ds(low, LANES)] = value.astype(BF16)

    def take(step, all_on):
        for i in range(PARTS):
            for way in range(2):
                h = ORDER[way][i]
                row = row_at(pos - step if way == 0 else pos + step)
                index = chips - step if way == 0 else step
                hop(way, step, h, row).wait_recv()
                if all_on or 2 * i < PARTS:
                    hop(way, step + 1, h, row).start()
                cross(index, h, row).start()

    def cross_arrived(index, place):
        other = 2 * chip_at(place) + 1 - core
        for h in range(PARTS):
            cross(index, h, other).wait_recv()

    def both_coeffs(step):
        def one(way, carry):
            index = (1 - way) * (chips - step) + way * step
            cross_arrived(index, pos + index)
            coeffs_of(pos + index)
            return carry
        lax.fori_loop(0, 2, one, 0)

    def gather_step(step, carry):
        take(step, True)

        @pl.when(step > 1)
        def _():
            both_coeffs(step - 1)
        return carry

    loads[1].wait()
    loads[3].wait()
    cross_arrived(0, pos)
    coeffs_of(pos)
    lax.fori_loop(1, half_ring - 1, gather_step, 0)
    take(half_ring - 1, False)
    both_coeffs(half_ring - 2)
    for i in range(PARTS // 2):
        for way in range(2):
            h = ORDER[way][i]
            hop(way, half_ring, h, row_at(pos + half_ring)).wait_recv()
            cross(half_ring, h, row_at(pos + half_ring)).start()
    both_coeffs(half_ring - 1)
    cross_arrived(half_ring, pos + half_ring)
    coeffs_of(pos + half_ring)

    def behind_me(target):
        return (target < me).astype(jnp.int32)

    def cross_sum(index):
        return send(
            partial.at[index, 1 - core], sib_in.at[index],
            rs_send.at[index], rs_recv.at[index], sibling)

    def fields_of(index):
        first = 2 * chip_at(pos + index)
        block = spread_all[pl.ds(first, 2)].reshape(2 * rows, depth)

        def one(w, carry):
            product = jnp.dot(block, right[w], preferred_element_type=F32)
            for i in range(2):
                @pl.when(behind_me(first + i) == w)
                def _():
                    partial[index, i] = product[i * rows:(i + 1) * rows, :]
            return carry

        lax.fori_loop(behind_me(first + 1), behind_me(first) + 1, one, 0)
        cross_sum(index).start()

    def both_fields(distance):
        def one(way, carry):
            fields_of((1 - way) * distance + way * (chips - distance))
            return carry
        lax.fori_loop(0, 2, one, 0)

    def ring(way, step, h):
        return send(
            ring_out.at[way, step - 1, pl.ds(h * half, half)],
            ring_in.at[way, step - 1, pl.ds(h * half, half)],
            r_send.at[way, step - 1, h], r_recv.at[way, step - 1, h],
            ahead if way == 0 else behind,
        )

    def own(index, h):
        at = pl.ds(h * half, half)
        return partial[index, core, at, :] + sib_in[index, at, :]

    def pass_on(step, way, h, fresh):
        distance = half_ring - (step - 1)
        index = distance if way == 0 else chips - distance
        at = pl.ds(h * half, half)
        total = own(index, h)
        if not fresh:
            ring(way, step - 1, h).wait_recv()
            total = total + ring_in[way, step - 2, at, :].astype(F32)
        ring_out[way, step - 1, at, :] = total.astype(ring_out.dtype)
        ring(way, step, h).start()

    def pass_all(step, turns, fresh):
        for i in turns:
            for way in range(2):
                pass_on(step, way, ORDER[way][i], fresh)

    loads[2].wait()
    loads[4].wait()
    fields_of(half_ring)
    both_fields(half_ring - 1)
    cross_sum(half_ring).wait_recv()
    pass_all(1, (0, 1), True)
    cross_sum(half_ring - 1).wait_recv()
    cross_sum(chips - half_ring + 1).wait_recv()
    pass_all(2, (2, 3), True)

    def more_fields(step, carry):
        both_fields(half_ring - step)
        return carry

    lax.fori_loop(2, half_ring, more_fields, 0)
    fields_of(0)
    pass_all(2, (0, 1), False)

    def reduce_step(step, carry):
        distance = half_ring - step + 1
        cross_sum(distance).wait_recv()
        cross_sum(chips - distance).wait_recv()
        pass_all(step, (2, 3, 0, 1), False)
        return carry

    lax.fori_loop(3, half_ring + 1, reduce_step, 0)

    loads[5].wait()
    for i in range(3):
        row = me + i - 1
        inside = jnp.logical_and(row >= 0, row < count)
        block = rows_all[(row + count) % count].astype(F32)
        beside[i, pl.ds(0, beams), :] = jnp.zeros((beams, width), F32)
        beside[i, pl.ds(beams, rows), :] = jnp.where(inside, block, 0.0)
        beside[i, pl.ds(beams + rows, beams), :] = jnp.zeros((beams, width), F32)
    near_acc[...] = jnp.zeros((rows, width), F32)

    def weights(offset):
        square = offset * offset
        return [((square + offset) // 2).astype(F32), (1 - square).astype(F32),
                ((square - offset) // 2).astype(F32)]

    def near_step(n, carry):
        by_row = weights(offsets[0, n])
        by_col = weights(offsets[1, n])
        picked = sum(beside[i] * by_row[i] for i in range(3))
        shifted = sum(
            picked[i * beams:i * beams + rows, :] * by_col[i] for i in range(3)).astype(BF16)
        near_acc[...] += jnp.dot(shifted, near_w[n], preferred_element_type=F32)
        return carry

    lax.fori_loop(0, nnear, near_step, 0)

    cross_sum(0).wait_recv()
    for h in range(PARTS):
        at = pl.ds(h * half, half)
        total = near_acc[at, :] + own(0, h)
        for way in range(2):
            ring(way, half_ring, h).wait_recv()
            total = total + ring_in[way, half_ring - 1, at, :].astype(F32)
        out[at, :] = total

    def sent(step, carry):
        for way in range(2):
            for h in range(PARTS):
                hop(way, step, h, me).wait_send()
                ring(way, half_ring + 1 - step, h).wait_send()
        return carry

    lax.fori_loop(1, half_ring, sent, 0)
    for way in range(2):
        for h in ORDER[way][:PARTS // 2]:
            hop(way, half_ring, h, me).wait_send()
            ring(way, 1, h).wait_send()

    def crossed(index, carry):
        for h in range(PARTS):
            cross(index, h, me).wait_send()
        cross_sum(index).wait_send()
        return carry

    lax.fori_loop(0, chips, crossed, 0)


def local(count, sources, far_left, far_right, ranks, near_blocks, near_offsets):
    _, ecol, beams, width = sources.shape
    slots, rank = far_left.shape[1], far_left.shape[2]
    nnear = near_blocks.shape[0]
    chips, rows = count // 2, ecol * beams
    half_ring = chips // 2
    depth = -(-slots * rank // 256) * 256
    dims = (count, ecol, beams, width, slots, rank, depth, nnear)
    flops = 2 * count * rows * depth * width * 2 + 2 * nnear * rows * width * width
    dma = pltpu.SemaphoreType.DMA
    anywhere = pl.BlockSpec(memory_space=pl.ANY)
    scalars = pl.BlockSpec(memory_space=pltpu.SMEM)
    fields = pl.pallas_call(
        functools.partial(kernel, dims),
        out_shape=jax.ShapeDtypeStruct((rows, width), F32),
        in_specs=[anywhere] * 4 + [scalars] * 2,
        out_specs=pl.BlockSpec(memory_space=pltpu.VMEM),
        scratch_shapes=[
            pltpu.VMEM((count, rows, width), BF16),
            pltpu.VMEM((2, depth, width), BF16),
            pltpu.VMEM((2, depth, width), BF16),
            pltpu.VMEM((nnear, width, width), BF16),
            pltpu.VMEM((2, 3 * rows, depth), F32),
            pltpu.VMEM((count, rows, depth), BF16),
            pltpu.VMEM((chips, 2, rows, width), F32),
            pltpu.VMEM((chips, rows, width), F32),
            pltpu.VMEM((2, half_ring, rows, width), BF16),
            pltpu.VMEM((2, half_ring, rows, width), BF16),
            pltpu.VMEM((3, rows + 2 * beams, width), F32),
            pltpu.VMEM((2, 8, depth), F32),
            pltpu.VMEM((rows, width), F32),
            dma((6,)),
            dma((2, half_ring, PARTS)),
            dma((2, half_ring, PARTS)),
            dma((chips, PARTS)),
            dma((chips, PARTS)),
            dma((2, half_ring, PARTS)),
            dma((2, half_ring, PARTS)),
            dma((chips,)),
            dma((chips,)),
        ],
        compiler_params=pltpu.CompilerParams(
            collective_id=0, has_side_effects=True, vmem_limit_bytes=62 * 2 ** 20),
        cost_estimate=pl.CostEstimate(
            flops=flops, bytes_accessed=13_000_000, transcendentals=0),
    )(
        sources.reshape(rows, width),
        far_left.reshape(2, slots * rank, width),
        far_right.reshape(2, slots * rank, width),
        near_blocks, ranks, near_offsets.T,
    )
    return fields.reshape(1, ecol, beams, width)


def solution(mesh):
    placed = (
        P(("grp", "row"), None, None, None),
        P(("grp", "row"), None, None, None),
        P(("grp", "row"), None, None, None),
        P(("grp", "row"), None),
        P("grp", None, None),
        P("grp", None),
    )
    return jax.shard_map(
        functools.partial(local, mesh.shape["row"]),
        mesh=mesh,
        in_specs=placed,
        out_specs=P(("grp", "row"), None, None, None),
        check_vma=False,
    )
```
